32 devices in a mesh: row: 8 (over y, x, core), col: 4 (over z).
Axes of the slice: x: 2, y: 2, z: 4, core: 2. Of those that a mesh axis runs over, the one named last changes fastest.
Arguments:
- traces: bfloat16 [4096, 782], P(('row', 'col')), may hold values from -60 to 60
- taps: float32 [16], replicated, may hold values from -1.5 to 1.5
Outputs:
- correlations: float32 [32, 4096, 4096], P(None, 'row', 'col')
The draws below stay inside these ranges and needn't reach their ends.
All inputs are finite; a program needn't handle non-finite values.
Results may differ from the reference program's by a relative error of at most 0.0036.
Values may be sent and summed in bfloat16 or wider, within the bound.
A program may use at most 256 MiB of HBM per device.

```python
import math
import jax
import jax.numpy as jnp
from jax import lax

C = 4096
TAPS = 16
LAGS = 32
M = 384
SR = 782
W = 353


def draw_traces(key, part):
    first, second = jax.random.split(key, 2)
    scales = jnp.exp(jax.random.uniform(first, (C, 1), jnp.float32, 0.0, math.log(10.0)))
    noise = jnp.clip(jax.random.normal(second, (C, SR), jnp.float32), -5.0, 5.0)
    values = scales * noise
    return values.astype(jnp.bfloat16)


def scatter_about(stream_key, shape, scale, limit, kind=jnp.bfloat16):
    drawn = scale * jax.random.normal(stream_key, shape, jnp.float32)
    return jnp.clip(drawn, min=-limit, max=limit).astype(kind)


def setup_inputs(seed: int = 0) -> dict:
    seeds = jax.random.split(jax.random.key(seed), 3)
    return {
        "traces": draw_traces(jax.random.fold_in(seeds[2], 71), 0),
        "taps": scatter_about(seeds[1], (TAPS,), TAPS ** -0.5, 1.5, jnp.float32),
    }


def whiten(traces, taps):
    samples = traces.astype(jnp.float32)
    decimated = jnp.zeros((samples.shape[0], M), jnp.float32)
    for k in range(TAPS):
        decimated = decimated + taps[k] * samples[:, k:k + 2 * M - 1:2]
    centred = decimated - lax.optimization_barrier(jnp.mean(decimated, axis=1, keepdims=True))
    spread = jnp.sqrt(lax.optimization_barrier(jnp.mean(centred * centred, axis=1, keepdims=True)) + 1e-06)
    return (centred / spread).astype(jnp.bfloat16)

def reference(traces, taps):
    whitened = whiten(traces, taps).astype(jnp.float32)
    left = whitened[:, :W]
    factor = 1.0 / math.sqrt(W)

    def one_lag(lag):
        right = lax.dynamic_slice_in_dim(whitened, lag, W, 1)
        return jnp.dot(left, right.T, precision=lax.Precision.HIGHEST, preferred_element_type=jnp.float32) * factor
    return lax.map(one_lag, jnp.arange(LAGS, dtype=jnp.int32))
```

```python
import functools
import math

import jax
import jax.numpy as jnp
from jax import lax
from jax.experimental import pallas as pl
from jax.experimental.pallas import tpu as pltpu
from jax.sharding import PartitionSpec as P

LAGS = 32
MESH = pl.DeviceIdType.MESH


def whiten(x_ref, taps_ref, count):
    taps = taps_ref.shape[0]
    tile = 128
    depth = 2 * tile + taps - 2
    m = lax.broadcasted_iota(jnp.int32, (depth, tile), 0)
    n = lax.broadcasted_iota(jnp.int32, (depth, tile), 1)
    offset = m - 2 * n
    band = jnp.zeros((depth, tile), jnp.float32)
    for k in range(taps):
        band = jnp.where(offset == k, taps_ref[k], band)
    high = band.astype(jnp.bfloat16)
    rest = band - high.astype(jnp.float32)
    middle = rest.astype(jnp.bfloat16)
    low = (rest - middle.astype(jnp.float32)).astype(jnp.bfloat16)
    pieces = []
    for t in range(count // tile):
        x = x_ref[:, 2 * tile * t : 2 * tile * t + depth]
        total = jnp.dot(x, low, preferred_element_type=jnp.float32)
        total += jnp.dot(x, middle, preferred_element_type=jnp.float32)
        total += jnp.dot(x, high, preferred_element_type=jnp.float32)
        pieces.append(total)
    decimated = jnp.concatenate(pieces, axis=1)
    centred = decimated - jnp.mean(decimated, axis=1, keepdims=True)
    spread = jnp.sqrt(jnp.mean(centred * centred, axis=1, keepdims=True) + 1e-06)
    return (centred / spread).astype(jnp.bfloat16)


def gather_kernel(R, C, count, x_ref, taps_ref, first, second, send1, recv1, send2, recv2, sendp, recvp):
    r = lax.axis_index("row")
    c = lax.axis_index("col")
    block = r * C + c
    to_r, to_c = lax.rem(block, R), lax.div(block, R)
    wanted = c * R + r
    from_r, from_c = lax.div(wanted, C), lax.rem(wanted, C)
    fixed = wanted == block

    barrier = pltpu.get_barrier_semaphore()

    def greet(row, col):
        pl.semaphore_signal(barrier, inc=1, device_id=(row, col), device_id_type=MESH)

    for k in range(1, R):
        greet(lax.rem(r + k, R), c)
    for k in range(1, C):
        greet(r, lax.rem(c + k, C))

    @pl.when(jnp.logical_not(fixed))
    def _():
        greet(to_r, to_c)
        greet(from_r, from_c)

    mine = whiten(x_ref, taps_ref, count)
    first[pl.ds(c, 1)] = mine[None]

    @pl.when(fixed)
    def _():
        second[pl.ds(r, 1)] = mine[None]

    pl.semaphore_wait(barrier, R - 1 + C - 1 + jnp.where(fixed, 0, 2))

    def swap():
        return pltpu.make_async_remote_copy(
            first.at[c], second.at[to_r], sendp, recvp, device_id=(to_r, to_c), device_id_type=MESH)

    def arrived_swap():
        return pltpu.make_async_remote_copy(
            first.at[c], second.at[r], sendp, recvp, device_id=(to_r, to_c), device_id_type=MESH)

    def col_copy(slot, col, way):
        return pltpu.make_async_remote_copy(
            first.at[slot], first.at[slot], send1.at[way, slot], recv1.at[slot],
            device_id=(r, col), device_id_type=MESH)

    def row_copy(slot, row, k):
        return pltpu.make_async_remote_copy(
            second.at[slot], second.at[slot], send2.at[k], recv2.at[slot],
            device_id=(row, c), device_id_type=MESH)

    @pl.when(jnp.logical_not(fixed))
    def _():
        swap().start()

    @pl.when(c + 1 < C)
    def _():
        col_copy(c, c + 1, 0).start()

    @pl.when(c >= 1)
    def _():
        col_copy(c, c - 1, 1).start()

    @pl.when(jnp.logical_not(fixed))
    def _():
        arrived_swap().wait_recv()

    half = R // 2
    core = lax.rem(r, 2)
    chip = lax.div(r, 2)
    partner = r + 1 - 2 * core
    for k in list(range(1, half)):
        row_copy(r, 2 * lax.rem(chip + k, half) + core, k).start()
    row_copy(r, partner, 0).start()

    for step in range(1, max(half, C)):
        if step < C:
            left, right = c - step, c + step

            @pl.when(left >= 0)
            def _():
                col_copy(left, c, 0).wait_recv()

                @pl.when(c + 1 < C)
                def _():
                    col_copy(left, c + 1, 0).start()

            @pl.when(right < C)
            def _():
                col_copy(right, c, 1).wait_recv()

                @pl.when(c >= 1)
                def _():
                    col_copy(right, c - 1, 1).start()

        if step < half:
            slot = 2 * lax.rem(chip + half - step, half) + core
            row_copy(slot, partner, 0).wait_recv()
            row_copy(slot, partner, half + step).start()

    for k in range(half):
        slot = 2 * lax.rem(chip + k, half) + 1 - core
        row_copy(slot, partner, 0).wait_recv()

    for k in range(half):
        row_copy(r, partner, k).wait_send()
    for k in range(1, half):
        row_copy(r, partner, half + k).wait_send()

    @pl.when(jnp.logical_not(fixed))
    def _():
        swap().wait_send()

    for slot in range(C):
        @pl.when(jnp.logical_and(slot <= c, c + 1 < C))
        def _():
            col_copy(slot, c + 1, 0).wait_send()

        @pl.when(jnp.logical_and(slot >= c, c >= 1))
        def _():
            col_copy(slot, c - 1, 1).wait_send()


def gather(R, C, count, traces, taps):
    rows = traces.shape[0]
    vmem = pl.BlockSpec(memory_space=pltpu.VMEM)
    return pl.pallas_call(
        functools.partial(gather_kernel, R, C, count),
        out_shape=(
            jax.ShapeDtypeStruct((C, rows, count), jnp.bfloat16),
            jax.ShapeDtypeStruct((R, rows, count), jnp.bfloat16),
        ),
        in_specs=[vmem, pl.BlockSpec(memory_space=pltpu.SMEM)],
        out_specs=(vmem, vmem),
        scratch_shapes=[
            pltpu.SemaphoreType.DMA((2, C)),
            pltpu.SemaphoreType.DMA((C,)),
            pltpu.SemaphoreType.DMA((R,)),
            pltpu.SemaphoreType.DMA((R,)),
            pltpu.SemaphoreType.DMA,
            pltpu.SemaphoreType.DMA,
        ],
        compiler_params=pltpu.CompilerParams(
            collective_id=0, has_side_effects=True, vmem_limit_bytes=32 * 1024 * 1024),
        name="whiten_gather",
    )(traces, taps)


def correlate_kernel(width, per_step, first, second, out, left, right, lagged):
    rows = left.shape[0]

    @pl.when(pl.program_id(0) == 0)
    def _():
        n = lax.broadcasted_iota(jnp.int32, left.shape, 1)
        left[...] = jnp.where(n < width, first[...].astype(jnp.float32), 0.0)
        right[...] = second[...].T

    scale = 1.0 / math.sqrt(width)
    x = left[...]
    for k in range(per_step):
        lagged[k * rows : (k + 1) * rows] = x.astype(jnp.bfloat16)
        x = pltpu.roll(x, 1, 1)
    left[...] = x
    product = jnp.dot(lagged[...], right[...], preferred_element_type=jnp.float32) * scale
    out[...] = product.reshape(out.shape)


def correlate(first, second, width, per_step=4):
    rows, count = first.shape
    columns = second.shape[0]
    return pl.pallas_call(
        functools.partial(correlate_kernel, width, per_step),
        out_shape=jax.ShapeDtypeStruct((LAGS, rows, columns), jnp.float32),
        grid=(LAGS // per_step,),
        in_specs=[
            pl.BlockSpec((rows, count), lambda s: (0, 0)),
            pl.BlockSpec((columns, count), lambda s: (0, 0)),
        ],
        out_specs=pl.BlockSpec((per_step, rows, columns), lambda s: (s, 0, 0)),
        scratch_shapes=[
            pltpu.VMEM((rows, count), jnp.float32),
            pltpu.VMEM((count, columns), jnp.bfloat16),
            pltpu.VMEM((per_step * rows, count), jnp.bfloat16),
        ],
        compiler_params=pltpu.CompilerParams(vmem_limit_bytes=48 * 1024 * 1024),
        cost_estimate=pl.CostEstimate(
            flops=2 * LAGS * rows * columns * count,
            bytes_accessed=4 * LAGS * rows * columns, transcendentals=0),
        name="correlate",
    )(first, second)


def whiten_columns(x, taps_ref, count):
    taps = taps_ref.shape[0]
    tile = 128
    depth = 2 * tile + taps - 2
    n = lax.broadcasted_iota(jnp.int32, (tile, depth), 0)
    m = lax.broadcasted_iota(jnp.int32, (tile, depth), 1)
    offset = m - 2 * n
    band = jnp.zeros((tile, depth), jnp.float32)
    for k in range(taps):
        band = jnp.where(offset == k, taps_ref[k], band)
    high = band.astype(jnp.bfloat16)
    rest = band - high.astype(jnp.float32)
    middle = rest.astype(jnp.bfloat16)
    low = (rest - middle.astype(jnp.float32)).astype(jnp.bfloat16)
    pieces = []
    for t in range(count // tile):
        part = x[2 * tile * t : 2 * tile * t + depth]
        total = jnp.dot(low, part, preferred_element_type=jnp.float32)
        total += jnp.dot(middle, part, preferred_element_type=jnp.float32)
        total += jnp.dot(high, part, preferred_element_type=jnp.float32)
        pieces.append(total)
    decimated = jnp.concatenate(pieces, axis=0)
    centred = decimated - jnp.mean(decimated, axis=0, keepdims=True)
    spread = jnp.sqrt(jnp.mean(centred * centred, axis=0, keepdims=True) + 1e-06)
    return (centred / spread).astype(jnp.bfloat16)


def spread_kernel(C, count, width, parts, rings, x_hbm, taps_hbm, first, second, column, x_ref, taps_ref,
                  in_sem, send_z, recv_z, send_p, recv_p, send_c, recv_c):
    r = lax.axis_index("row")
    c = lax.axis_index("col")
    core = lax.rem(r, 2)
    place = lax.div(r, 2)
    px, py = lax.rem(place, 2), lax.div(place, 2)
    beside = 2 * (2 * py + 1 - px) + core
    across = 2 * (2 * (1 - py) + px) + core
    partner = r + 1 - 2 * core
    source = place == c
    relay = jnp.logical_not(source)
    same_x, same_y = px == lax.rem(c, 2), py == lax.div(c, 2)
    apart_x, apart_y = jnp.logical_not(same_x), jnp.logical_not(same_y)
    corner = jnp.logical_and(apart_x, apart_y)
    hop_one = jnp.logical_or(
        jnp.logical_and(core == 0, jnp.logical_and(same_y, apart_x)),
        jnp.logical_and(core == 1, jnp.logical_and(same_x, apart_y)))
    ways = (jnp.where(core == 0, beside, across), jnp.where(core == 0, across, beside))
    mine, other = core * C, (1 - core) * C
    depth = count // parts
    order = [sorted(range(C), key=lambda z: (abs(z - i), z)) for i in range(C)]
    slots = [sum(jnp.where(c == i, order[i][n], 0) for i in range(C)) for n in range(C)]

    read_x = pltpu.make_async_copy(x_hbm, x_ref, in_sem.at[0])
    read_taps = pltpu.make_async_copy(taps_hbm, taps_ref, in_sem.at[1])
    read_x.start()
    read_taps.start()

    barrier = pltpu.get_barrier_semaphore()

    def greet(row, col):
        pl.semaphore_signal(barrier, inc=1, device_id=(row, col), device_id_type=MESH)

    greet(partner, c)
    greet(beside, c)
    greet(across, c)
    for k in range(1, C):
        greet(r, lax.rem(c + k, C))

    read_taps.wait()
    read_x.wait()
    block = whiten_columns(x_ref[...], taps_ref, count)
    column[pl.ds(c, 1)] = block[None]

    @pl.when(source)
    def _():
        second[pl.ds(mine + c, 1)] = block[None]

    pl.semaphore_wait(barrier, 3 + C - 1)

    def rows_of(part):
        return pl.ds(pl.multiple_of(part * depth, depth), depth)

    def z_copy(slot, part, col):
        ref = column.at[slot, rows_of(part)]
        return pltpu.make_async_remote_copy(
            ref, ref, send_z.at[col, part], recv_z.at[slot, part],
            device_id=(r, col), device_id_type=MESH)

    def plane_copy(buffer, index, slot, part, way):
        return pltpu.make_async_remote_copy(
            buffer.at[index, rows_of(part)], second.at[mine + slot, rows_of(part)],
            send_p.at[way, slot, part], recv_p.at[slot, part],
            device_id=(ways[way], c), device_id_type=MESH)

    def core_copy(buffer, index, slot, part):
        return pltpu.make_async_remote_copy(
            buffer.at[index, rows_of(part)], second.at[mine + slot, rows_of(part)],
            send_c.at[slot, part], recv_c.at[slot, part],
            device_id=(partner, c), device_id_type=MESH)

    def core_arrived(slot, part):
        ref = second.at[other + slot, rows_of(part)]
        return pltpu.make_async_remote_copy(
            ref, ref, send_c.at[slot, part], recv_c.at[slot, part],
            device_id=(partner, c), device_id_type=MESH)

    def turn(slot):
        block = column[pl.ds(slot, 1)][0].astype(jnp.float32)
        n = lax.broadcasted_iota(jnp.int32, block.shape, 0)
        rows = block.shape[1]
        turned = jnp.where(n < width, block, 0.0).T.astype(jnp.bfloat16)
        first[pl.ds(pl.multiple_of(slot * rows, rows), rows)] = turned

    def spread_out(n, part):
        plane_copy(column, slots[n], slots[n], part, 0).start()
        if n >= rings:
            plane_copy(column, slots[n], slots[n], part, 1).start()
        core_copy(column, slots[n], slots[n], part).start()

    @pl.when(source)
    def _():
        @pl.loop(0, parts)
        def _(part):
            spread_out(0, part)

    for k in range(C):
        col = lax.rem(place + k, C)

        @pl.when(col != c)
        def _():
            @pl.loop(0, parts)
            def _(part):
                z_copy(c, part, col).start()

    turn(c)

    @pl.when(source)
    def _():
        for n in range(1, C):
            @pl.loop(0, parts)
            def _(part):
                z_copy(slots[n], part, c).wait_recv()
                spread_out(n, part)

            second[pl.ds(mine + slots[n], 1)] = column[pl.ds(slots[n], 1)]

    @pl.when(relay)
    def _():
        for n in range(C):
            @pl.loop(0, parts)
            def _(part):
                plane_copy(column, slots[n], slots[n], part, 0).wait_recv()

                @pl.when(hop_one)
                def _():
                    plane_copy(second, mine + slots[n], slots[n], part, 1).start()

                if n < rings:
                    @pl.when(corner)
                    def _():
                        plane_copy(second, mine + slots[n], slots[n], part, 0).start()

                core_copy(second, mine + slots[n], slots[n], part).start()

        for n in range(1, C):
            @pl.loop(0, parts)
            def _(part):
                z_copy(slots[n], part, c).wait_recv()

    for n in range(1, C):
        turn(slots[n])

    @pl.loop(0, parts)
    def _(part):
        for n in range(C):
            core_arrived(slots[n], part).wait_recv()
            core_copy(column, slots[n], slots[n], part).wait_send()

            @pl.when(jnp.logical_or(source, corner) if n < rings else source)
            def _():
                plane_copy(column, slots[n], slots[n], part, 0).wait_send()

            @pl.when(hop_one if n < rings else jnp.logical_or(source, hop_one))
            def _():
                plane_copy(column, slots[n], slots[n], part, 1).wait_send()

        for k in range(1, C):
            z_copy(c, part, lax.rem(c + k, C)).wait_send()


def spread(C, count, width, columns, taps, parts=4, rings=0):
    rows = columns.shape[1]
    vmem = pl.BlockSpec(memory_space=pltpu.VMEM)
    hbm = pl.BlockSpec(memory_space=pltpu.HBM)
    return pl.pallas_call(
        functools.partial(spread_kernel, C, count, width, parts, rings),
        out_shape=(
            jax.ShapeDtypeStruct((C * rows, count), jnp.bfloat16),
            jax.ShapeDtypeStruct((2 * C, count, rows), jnp.bfloat16),
        ),
        in_specs=[hbm, hbm],
        out_specs=(vmem, vmem),
        scratch_shapes=[
            pltpu.VMEM((C, count, rows), jnp.bfloat16),
            pltpu.VMEM(columns.shape, columns.dtype),
            pltpu.SMEM(taps.shape, taps.dtype),
            pltpu.SemaphoreType.DMA((2,)),
            pltpu.SemaphoreType.DMA((C, parts)),
            pltpu.SemaphoreType.DMA((C, parts)),
            pltpu.SemaphoreType.DMA((2, C, parts)),
            pltpu.SemaphoreType.DMA((C, parts)),
            pltpu.SemaphoreType.DMA((C, parts)),
            pltpu.SemaphoreType.DMA((C, parts)),
        ],
        compiler_params=pltpu.CompilerParams(
            collective_id=1, has_side_effects=True, vmem_limit_bytes=16 * 1024 * 1024),
        name="whiten_spread",
    )(columns, taps)


def correlate_slots_kernel(width, per_step, first, second, out, left, right, lagged, done, sem):
    rows = left.shape[0]
    steps = LAGS // per_step
    slots = done.shape[0]
    left[...] = first[...].astype(jnp.float32)
    for k in range(second.shape[0]):
        right[:, k * second.shape[2] : (k + 1) * second.shape[2]] = second[k]
    scale = 1.0 / math.sqrt(width)

    def store(step, slot):
        return pltpu.make_async_copy(
            done.at[slot], out.at[pl.ds(step * per_step, per_step)], sem.at[slot])

    @pl.loop(0, steps)
    def _(step):
        slot = lax.rem(step, slots)

        @pl.when(step >= slots)
        def _():
            store(step - slots, slot).wait()

        x = left[...]
        for k in range(per_step):
            lagged[k * rows : (k + 1) * rows] = x.astype(jnp.bfloat16)
            x = pltpu.roll(x, 1, 1)
        left[...] = x
        product = jnp.dot(lagged[...], right[...], preferred_element_type=jnp.float32) * scale
        done[pl.ds(slot, 1)] = product.reshape((1,) + done.shape[1:])
        store(step, slot).start()

    for step in range(steps - slots, steps):
        store(step, step % slots).wait()


def correlate_slots(first, second, width, per_step=2, slots=3):
    rows, count = first.shape
    columns = second.shape[0] * second.shape[2]
    vmem = pl.BlockSpec(memory_space=pltpu.VMEM)
    return pl.pallas_call(
        functools.partial(correlate_slots_kernel, width, per_step),
        out_shape=jax.ShapeDtypeStruct((LAGS, rows, columns), jnp.float32),
        in_specs=[vmem, vmem],
        out_specs=pl.BlockSpec(memory_space=pl.ANY),
        scratch_shapes=[
            pltpu.VMEM((rows, count), jnp.float32),
            pltpu.VMEM((count, columns), jnp.bfloat16),
            pltpu.VMEM((per_step * rows, count), jnp.bfloat16),
            pltpu.VMEM((slots, per_step, rows, columns), jnp.float32),
            pltpu.SemaphoreType.DMA((slots,)),
        ],
        compiler_params=pltpu.CompilerParams(vmem_limit_bytes=48 * 1024 * 1024),
        cost_estimate=pl.CostEstimate(
            flops=2 * LAGS * rows * columns * count,
            bytes_accessed=4 * LAGS * rows * columns, transcendentals=0),
        name="correlate",
    )(first, second)


def solution(mesh):
    R, C = mesh.shape["row"], mesh.shape["col"]

    def on_device(traces, taps):
        count = (traces.shape[1] - taps.shape[0] + 2) // 2
        width = count - LAGS + 1
        if (R, C) == (8, 4) and traces.shape[0] == 128:
            first, second = spread(C, count, width, traces.T, taps)
            return correlate_slots(first, second, width)
        first, second = gather(R, C, count, traces, taps)
        first = first.reshape(-1, count)
        second = second.reshape(-1, count)
        return correlate(first, second, width)

    placed = (P(("row", "col"), None), P())
    return jax.shard_map(
        on_device, mesh=mesh, in_specs=placed, out_specs=P(None, "row", "col"), check_vma=False
    )
```

```python
import functools
import math

import jax
import jax.numpy as jnp
from jax import lax
from jax.experimental import pallas as pl
from jax.experimental.pallas import tpu as pltpu
from jax.sharding import PartitionSpec as P

LAGS = 32
MESH = pl.DeviceIdType.MESH


def whiten(x_ref, taps_ref, count):
    taps = taps_ref.shape[0]
    tile = 128
    depth = 2 * tile + taps - 2
    m = lax.broadcasted_iota(jnp.int32, (depth, tile), 0)
    n = lax.broadcasted_iota(jnp.int32, (depth, tile), 1)
    offset = m - 2 * n
    band = jnp.zeros((depth, tile), jnp.float32)
    for k in range(taps):
        band = jnp.where(offset == k, taps_ref[k], band)
    high = band.astype(jnp.bfloat16)
    rest = band - high.astype(jnp.float32)
    middle = rest.astype(jnp.bfloat16)
    low = (rest - middle.astype(jnp.float32)).astype(jnp.bfloat16)
    pieces = []
    for t in range(count // tile):
        x = x_ref[:, 2 * tile * t : 2 * tile * t + depth]
        total = jnp.dot(x, low, preferred_element_type=jnp.float32)
        total += jnp.dot(x, middle, preferred_element_type=jnp.float32)
        total += jnp.dot(x, high, preferred_element_type=jnp.float32)
        pieces.append(total)
    decimated = jnp.concatenate(pieces, axis=1)
    centred = decimated - jnp.mean(decimated, axis=1, keepdims=True)
    spread = jnp.sqrt(jnp.mean(centred * centred, axis=1, keepdims=True) + 1e-06)
    return (centred / spread).astype(jnp.bfloat16)


def gather_kernel(R, C, count, x_ref, taps_ref, first, second, send1, recv1, send2, recv2, sendp, recvp):
    r = lax.axis_index("row")
    c = lax.axis_index("col")
    block = r * C + c
    to_r, to_c = lax.rem(block, R), lax.div(block, R)
    wanted = c * R + r
    from_r, from_c = lax.div(wanted, C), lax.rem(wanted, C)
    fixed = wanted == block

    barrier = pltpu.get_barrier_semaphore()

    def greet(row, col):
        pl.semaphore_signal(barrier, inc=1, device_id=(row, col), device_id_type=MESH)

    for k in range(1, R):
        greet(lax.rem(r + k, R), c)
    for k in range(1, C):
        greet(r, lax.rem(c + k, C))

    @pl.when(jnp.logical_not(fixed))
    def _():
        greet(to_r, to_c)
        greet(from_r, from_c)

    mine = whiten(x_ref, taps_ref, count)
    first[pl.ds(c, 1)] = mine[None]

    @pl.when(fixed)
    def _():
        second[pl.ds(r, 1)] = mine[None]

    pl.semaphore_wait(barrier, R - 1 + C - 1 + jnp.where(fixed, 0, 2))

    def swap():
        return pltpu.make_async_remote_copy(
            first.at[c], second.at[to_r], sendp, recvp, device_id=(to_r, to_c), device_id_type=MESH)

    def arrived_swap():
        return pltpu.make_async_remote_copy(
            first.at[c], second.at[r], sendp, recvp, device_id=(to_r, to_c), device_id_type=MESH)

    def col_copy(slot, col, way):
        return pltpu.make_async_remote_copy(
            first.at[slot], first.at[slot], send1.at[way, slot], recv1.at[slot],
            device_id=(r, col), device_id_type=MESH)

    def row_copy(slot, row, k):
        return pltpu.make_async_remote_copy(
            second.at[slot], second.at[slot], send2.at[k], recv2.at[slot],
            device_id=(row, c), device_id_type=MESH)

    @pl.when(jnp.logical_not(fixed))
    def _():
        swap().start()

    @pl.when(c + 1 < C)
    def _():
        col_copy(c, c + 1, 0).start()

    @pl.when(c >= 1)
    def _():
        col_copy(c, c - 1, 1).start()

    @pl.when(jnp.logical_not(fixed))
    def _():
        arrived_swap().wait_recv()

    half = R // 2
    core = lax.rem(r, 2)
    chip = lax.div(r, 2)
    partner = r + 1 - 2 * core
    for k in list(range(1, half)):
        row_copy(r, 2 * lax.rem(chip + k, half) + core, k).start()
    row_copy(r, partner, 0).start()

    for step in range(1, max(half, C)):
        if step < C:
            left, right = c - step, c + step

            @pl.when(left >= 0)
            def _():
                col_copy(left, c, 0).wait_recv()

                @pl.when(c + 1 < C)
                def _():
                    col_copy(left, c + 1, 0).start()

            @pl.when(right < C)
            def _():
                col_copy(right, c, 1).wait_recv()

                @pl.when(c >= 1)
                def _():
                    col_copy(right, c - 1, 1).start()

        if step < half:
            slot = 2 * lax.rem(chip + half - step, half) + core
            row_copy(slot, partner, 0).wait_recv()
            row_copy(slot, partner, half + step).start()

    for k in range(half):
        slot = 2 * lax.rem(chip + k, half) + 1 - core
        row_copy(slot, partner, 0).wait_recv()

    for k in range(half):
        row_copy(r, partner, k).wait_send()
    for k in range(1, half):
        row_copy(r, partner, half + k).wait_send()

    @pl.when(jnp.logical_not(fixed))
    def _():
        swap().wait_send()

    for slot in range(C):
        @pl.when(jnp.logical_and(slot <= c, c + 1 < C))
        def _():
            col_copy(slot, c + 1, 0).wait_send()

        @pl.when(jnp.logical_and(slot >= c, c >= 1))
        def _():
            col_copy(slot, c - 1, 1).wait_send()


def gather(R, C, count, traces, taps):
    rows = traces.shape[0]
    vmem = pl.BlockSpec(memory_space=pltpu.VMEM)
    return pl.pallas_call(
        functools.partial(gather_kernel, R, C, count),
        out_shape=(
            jax.ShapeDtypeStruct((C, rows, count), jnp.bfloat16),
            jax.ShapeDtypeStruct((R, rows, count), jnp.bfloat16),
        ),
        in_specs=[vmem, pl.BlockSpec(memory_space=pltpu.SMEM)],
        out_specs=(vmem, vmem),
        scratch_shapes=[
            pltpu.SemaphoreType.DMA((2, C)),
            pltpu.SemaphoreType.DMA((C,)),
            pltpu.SemaphoreType.DMA((R,)),
            pltpu.SemaphoreType.DMA((R,)),
            pltpu.SemaphoreType.DMA,
            pltpu.SemaphoreType.DMA,
        ],
        compiler_params=pltpu.CompilerParams(
            collective_id=0, has_side_effects=True, vmem_limit_bytes=32 * 1024 * 1024),
        name="whiten_gather",
    )(traces, taps)


def correlate_kernel(width, per_step, first, second, out, left, right, lagged):
    rows = left.shape[0]

    @pl.when(pl.program_id(0) == 0)
    def _():
        n = lax.broadcasted_iota(jnp.int32, left.shape, 1)
        left[...] = jnp.where(n < width, first[...].astype(jnp.float32), 0.0)
        right[...] = second[...].T

    scale = 1.0 / math.sqrt(width)
    x = left[...]
    for k in range(per_step):
        lagged[k * rows : (k + 1) * rows] = x.astype(jnp.bfloat16)
        x = pltpu.roll(x, 1, 1)
    left[...] = x
    product = jnp.dot(lagged[...], right[...], preferred_element_type=jnp.float32) * scale
    out[...] = product.reshape(out.shape)


def correlate(first, second, width, per_step=4):
    rows, count = first.shape
    columns = second.shape[0]
    return pl.pallas_call(
        functools.partial(correlate_kernel, width, per_step),
        out_shape=jax.ShapeDtypeStruct((LAGS, rows, columns), jnp.float32),
        grid=(LAGS // per_step,),
        in_specs=[
            pl.BlockSpec((rows, count), lambda s: (0, 0)),
            pl.BlockSpec((columns, count), lambda s: (0, 0)),
        ],
        out_specs=pl.BlockSpec((per_step, rows, columns), lambda s: (s, 0, 0)),
        scratch_shapes=[
            pltpu.VMEM((rows, count), jnp.float32),
            pltpu.VMEM((count, columns), jnp.bfloat16),
            pltpu.VMEM((per_step * rows, count), jnp.bfloat16),
        ],
        compiler_params=pltpu.CompilerParams(vmem_limit_bytes=48 * 1024 * 1024),
        cost_estimate=pl.CostEstimate(
            flops=2 * LAGS * rows * columns * count,
            bytes_accessed=4 * LAGS * rows * columns, transcendentals=0),
        name="correlate",
    )(first, second)


def whiten_columns(x, taps_ref, count):
    taps = taps_ref.shape[0]
    tile = 128
    depth = 2 * tile + taps - 2
    n = lax.broadcasted_iota(jnp.int32, (tile, depth), 0)
    m = lax.broadcasted_iota(jnp.int32, (tile, depth), 1)
    offset = m - 2 * n
    band = jnp.zeros((tile, depth), jnp.float32)
    for k in range(taps):
        band = jnp.where(offset == k, taps_ref[k], band)
    high = band.astype(jnp.bfloat16)
    rest = band - high.astype(jnp.float32)
    middle = rest.astype(jnp.bfloat16)
    low = (rest - middle.astype(jnp.float32)).astype(jnp.bfloat16)
    pieces = []
    for t in range(count // tile):
        part = x[2 * tile * t : 2 * tile * t + depth]
        total = jnp.dot(low, part, preferred_element_type=jnp.float32)
        total += jnp.dot(middle, part, preferred_element_type=jnp.float32)
        total += jnp.dot(high, part, preferred_element_type=jnp.float32)
        pieces.append(total)
    decimated = jnp.concatenate(pieces, axis=0)
    centred = decimated - jnp.mean(decimated, axis=0, keepdims=True)
    spread = jnp.sqrt(jnp.mean(centred * centred, axis=0, keepdims=True) + 1e-06)
    return (centred / spread).astype(jnp.bfloat16)


def spread_kernel(C, count, width, parts, x_hbm, taps_hbm, first, second, column, carry, x_ref, taps_ref,
                  in_sem, send_z, recv_z, send_p, recv_p, send_c, recv_c,
                  send_a, recv_a, send_b):
    r = lax.axis_index("row")
    c = lax.axis_index("col")
    core = lax.rem(r, 2)
    place = lax.div(r, 2)
    px, py = lax.rem(place, 2), lax.div(place, 2)
    beside = 2 * (2 * py + 1 - px) + core
    across = 2 * (2 * (1 - py) + px) + core
    partner = r + 1 - 2 * core
    source = place == c
    sx, sy = lax.rem(c, 2), lax.div(c, 2)
    same_x, same_y = px == sx, py == sy
    corner = jnp.logical_and(jnp.logical_not(same_x), jnp.logical_not(same_y))
    near = jnp.logical_and(jnp.logical_not(source), jnp.logical_not(corner))
    relay_y = jnp.logical_and(jnp.logical_and(near, same_y), core == 0)
    relay_x = jnp.logical_and(jnp.logical_and(near, same_x), core == 1)
    far = C - 1 - c
    ends = jnp.logical_or(c == 0, far == 0)
    starts = jnp.logical_and(ends, corner)
    carries = jnp.logical_and(ends, jnp.logical_not(corner))
    relay = jnp.logical_or(relay_x, relay_y)
    passes = jnp.where(core == 0, across, beside)
    along_x = jnp.logical_and(near, same_y)
    along_y = jnp.logical_and(near, same_x)
    mine, other = core * C, (1 - core) * C
    depth = count // parts

    read_x = pltpu.make_async_copy(x_hbm, x_ref, in_sem.at[0])
    read_taps = pltpu.make_async_copy(taps_hbm, taps_ref, in_sem.at[1])
    read_x.start()
    read_taps.start()

    barrier = pltpu.get_barrier_semaphore()

    def greet(row, col):
        pl.semaphore_signal(barrier, inc=1, device_id=(row, col), device_id_type=MESH)

    greet(partner, c)

    @pl.when(jnp.logical_or(along_x, jnp.logical_and(along_y, ends)))
    def _():
        greet(beside, c)

    @pl.when(jnp.logical_or(along_y, jnp.logical_and(along_x, ends)))
    def _():
        greet(across, c)

    @pl.when(corner)
    def _():
        greet(passes, c)

    @pl.when(c + 1 < C)
    def _():
        greet(r, c + 1)

    @pl.when(c >= 1)
    def _():
        greet(r, c - 1)

    @pl.when(jnp.logical_and(ends, jnp.logical_not(source)))
    def _():
        greet(r, far)

    @pl.when(jnp.logical_and(ends, source))
    def _():
        greet(2 * far + core, c)

    read_taps.wait()
    read_x.wait()
    block = whiten_columns(x_ref[...], taps_ref, count)
    column[pl.ds(c, 1)] = block[None]

    @pl.when(source)
    def _():
        second[pl.ds(mine + c, 1)] = block[None]

    pl.semaphore_wait(
        barrier, 1 + jnp.where(c + 1 < C, 1, 0) + jnp.where(c >= 1, 1, 0) + jnp.where(carries, 1, 0)
        + jnp.where(starts, 3, 0) + jnp.where(source, 2, 0) + jnp.where(relay, 1, 0))

    def rows_of(part):
        return pl.ds(pl.multiple_of(part * depth, depth), depth)

    def z_copy(slot, part, col, way):
        ref = column.at[slot, rows_of(part)]
        return pltpu.make_async_remote_copy(
            ref, ref, send_z.at[way, slot, part], recv_z.at[slot, part],
            device_id=(r, col), device_id_type=MESH)

    def plane_copy(buffer, index, slot, part, row, way):
        return pltpu.make_async_remote_copy(
            buffer.at[index, rows_of(part)], second.at[mine + slot, rows_of(part)],
            send_p.at[way, slot, part], recv_p.at[slot, part],
            device_id=(row, c), device_id_type=MESH)

    def core_copy(buffer, index, slot, part):
        return pltpu.make_async_remote_copy(
            buffer.at[index, rows_of(part)], second.at[mine + slot, rows_of(part)],
            send_c.at[slot, part], recv_c.at[slot, part],
            device_id=(partner, c), device_id_type=MESH)

    def core_arrived(slot, part):
        ref = second.at[other + slot, rows_of(part)]
        return pltpu.make_async_remote_copy(
            ref, ref, send_c.at[slot, part], recv_c.at[slot, part],
            device_id=(partner, c), device_id_type=MESH)

    def carry_start(part, way):
        ref = column.at[c, rows_of(part)]
        return pltpu.make_async_remote_copy(
            ref, carry.at[rows_of(part)], send_a.at[way, part], recv_a.at[part],
            device_id=((beside, across, 2 * c + core)[way], c), device_id_type=MESH)

    def carry_on(part):
        return pltpu.make_async_remote_copy(
            carry.at[rows_of(part)], second.at[mine + c, rows_of(part)], send_b.at[part], recv_p.at[c, part],
            device_id=(r, far), device_id_type=MESH)

    def spread_out(slot, part, step):
        @pl.when(source)
        def _():
            if step < C - 1:
                plane_copy(column, slot, slot, part, beside, 0).start()
                plane_copy(column, slot, slot, part, across, 1).start()
            core_copy(column, slot, slot, part).start()

    def hear(slot, part, step):
        plane_copy(column, slot, slot, part, beside, 0).wait_recv()

        if step < C - 1:
            @pl.when(relay_y)
            def _():
                plane_copy(second, mine + slot, slot, part, across, 1).start()

            @pl.when(relay_x)
            def _():
                plane_copy(second, mine + slot, slot, part, beside, 0).start()

        core_copy(second, mine + slot, slot, part).start()

    def each(step, act):
        if step == 0:
            act(c)
            return

        @pl.when(c - step >= 0)
        def _():
            act(c - step)

        @pl.when(c + step < C)
        def _():
            act(c + step)

    def keep(slot):
        @pl.when(source)
        def _():
            second[pl.ds(mine + slot, 1)] = column[pl.ds(slot, 1)]

    def turn(slot):
        block = column[pl.ds(slot, 1)][0].astype(jnp.float32)
        n = lax.broadcasted_iota(jnp.int32, block.shape, 0)
        rows = block.shape[1]
        turned = jnp.where(n < width, block, 0.0).T.astype(jnp.bfloat16)
        first[pl.ds(pl.multiple_of(slot * rows, rows), rows)] = turned

    @pl.loop(0, parts)
    def _(part):
        @pl.when(c + 1 < C)
        def _():
            z_copy(c, part, c + 1, 0).start()

        @pl.when(c >= 1)
        def _():
            z_copy(c, part, c - 1, 1).start()

        spread_out(c, part, 0)

        @pl.when(starts)
        def _():
            for way in range(3):
                carry_start(part, way).start()

    turn(c)

    for step in range(1, C + 2):
        @pl.loop(0, parts)
        def _(part):
            if step < C:
                @pl.when(c - step >= 0)
                def _():
                    z_copy(c - step, part, c, 0).wait_recv()

                    @pl.when(c + 1 < C)
                    def _():
                        z_copy(c - step, part, c + 1, 0).start()

                    spread_out(c - step, part, step)

                @pl.when(c + step < C)
                def _():
                    z_copy(c + step, part, c, 1).wait_recv()

                    @pl.when(c >= 1)
                    def _():
                        z_copy(c + step, part, c - 1, 1).start()

                    spread_out(c + step, part, step)

            if step - 1 < C:
                @pl.when(near)
                def _():
                    each(step - 1, lambda slot: hear(slot, part, step - 1))

            if step >= 2:
                @pl.when(corner)
                def _():
                    each(step - 2, lambda slot: hear(slot, part, step - 2))

        if step == 1:
            @pl.when(carries)
            def _():
                @pl.loop(0, parts)
                def _(part):
                    carry_start(part, 0).wait_recv()
                    carry_on(part).start()

        if step < C:
            each(step, keep)
            each(step, turn)

    @pl.loop(0, C * parts)
    def _(k):
        slot, part = lax.div(k, parts), lax.rem(k, parts)
        core_arrived(slot, part).wait_recv()
        core_copy(column, slot, slot, part).wait_send()

        near_slot = jnp.logical_and(slot - c < C - 1, c - slot < C - 1)

        @pl.when(jnp.logical_and(near_slot, jnp.logical_or(source, relay_x)))
        def _():
            plane_copy(column, slot, slot, part, beside, 0).wait_send()

        @pl.when(jnp.logical_and(near_slot, jnp.logical_or(source, relay_y)))
        def _():
            plane_copy(column, slot, slot, part, across, 1).wait_send()

        @pl.when(jnp.logical_and(slot <= c, c + 1 < C))
        def _():
            z_copy(slot, part, c + 1, 0).wait_send()

        @pl.when(jnp.logical_and(slot >= c, c >= 1))
        def _():
            z_copy(slot, part, c - 1, 1).wait_send()

    @pl.loop(0, parts)
    def _(part):
        @pl.when(starts)
        def _():
            for way in range(3):
                carry_start(part, way).wait_send()

        @pl.when(carries)
        def _():
            carry_on(part).wait_send()


def spread(C, count, width, columns, taps, parts=2):
    rows = columns.shape[1]
    vmem = pl.BlockSpec(memory_space=pltpu.VMEM)
    hbm = pl.BlockSpec(memory_space=pltpu.HBM)
    return pl.pallas_call(
        functools.partial(spread_kernel, C, count, width, parts),
        out_shape=(
            jax.ShapeDtypeStruct((C * rows, count), jnp.bfloat16),
            jax.ShapeDtypeStruct((2 * C, count, rows), jnp.bfloat16),
        ),
        in_specs=[hbm, hbm],
        out_specs=(vmem, vmem),
        scratch_shapes=[
            pltpu.VMEM((C, count, rows), jnp.bfloat16),
            pltpu.VMEM((count, rows), jnp.bfloat16),
            pltpu.VMEM(columns.shape, columns.dtype),
            pltpu.SMEM(taps.shape, taps.dtype),
            pltpu.SemaphoreType.DMA((2,)),
            pltpu.SemaphoreType.DMA((2, C, parts)),
            pltpu.SemaphoreType.DMA((C, parts)),
            pltpu.SemaphoreType.DMA((2, C, parts)),
            pltpu.SemaphoreType.DMA((C, parts)),
            pltpu.SemaphoreType.DMA((C, parts)),
            pltpu.SemaphoreType.DMA((C, parts)),
            pltpu.SemaphoreType.DMA((3, parts)),
            pltpu.SemaphoreType.DMA((parts,)),
            pltpu.SemaphoreType.DMA((parts,)),
        ],
        compiler_params=pltpu.CompilerParams(
            collective_id=1, has_side_effects=True, vmem_limit_bytes=16 * 1024 * 1024),
        name="whiten_spread",
    )(columns, taps)


def correlate_slots_kernel(width, per_step, first, second, out, left, right, lagged, done, single, sem, sem_single):
    rows = left.shape[0]
    steps = LAGS // per_step - 2
    slots = done.shape[0]
    left[...] = first[...].astype(jnp.float32)
    for k in range(second.shape[0]):
        right[:, k * second.shape[2] : (k + 1) * second.shape[2]] = second[k]
    scale = 1.0 / math.sqrt(width)

    def products(lags):
        x = left[...]
        for k in range(lags):
            lagged[k * rows : (k + 1) * rows] = x.astype(jnp.bfloat16)
            x = pltpu.roll(x, 1, 1)
        left[...] = x
        result = jnp.dot(lagged[: lags * rows], right[...], preferred_element_type=jnp.float32) * scale
        return result.reshape((lags,) + done.shape[2:])

    def store(step, slot):
        return pltpu.make_async_copy(
            done.at[slot], out.at[pl.ds(per_step * (step + 1), per_step)], sem.at[slot])

    def store_single(lag, slot):
        return pltpu.make_async_copy(single.at[slot], out.at[lag], sem_single.at[slot])

    for k in range(per_step):
        single[k] = products(1)[0]
        store_single(k, k).start()

    @pl.loop(0, steps)
    def _(step):
        slot = lax.rem(step, slots)

        @pl.when(step >= slots)
        def _():
            store(step - slots, slot).wait()

        done[pl.ds(slot, 1)] = products(per_step)[None]
        store(step, slot).start()

    for k in range(per_step):
        store_single(k, k).wait()
        single[k] = products(1)[0]
        store_single(LAGS - per_step + k, k).start()
    for step in range(steps - slots, steps):
        store(step, step % slots).wait()
    for k in range(per_step):
        store_single(LAGS - per_step + k, k).wait()


def correlate_slots(first, second, width, per_step=2, slots=3):
    rows, count = first.shape
    columns = second.shape[0] * second.shape[2]
    vmem = pl.BlockSpec(memory_space=pltpu.VMEM)
    return pl.pallas_call(
        functools.partial(correlate_slots_kernel, width, per_step),
        out_shape=jax.ShapeDtypeStruct((LAGS, rows, columns), jnp.float32),
        in_specs=[vmem, vmem],
        out_specs=pl.BlockSpec(memory_space=pl.ANY),
        scratch_shapes=[
            pltpu.VMEM((rows, count), jnp.float32),
            pltpu.VMEM((count, columns), jnp.bfloat16),
            pltpu.VMEM((per_step * rows, count), jnp.bfloat16),
            pltpu.VMEM((slots, per_step, rows, columns), jnp.float32),
            pltpu.VMEM((per_step, rows, columns), jnp.float32),
            pltpu.SemaphoreType.DMA((slots,)),
            pltpu.SemaphoreType.DMA((per_step,)),
        ],
        compiler_params=pltpu.CompilerParams(vmem_limit_bytes=48 * 1024 * 1024),
        cost_estimate=pl.CostEstimate(
            flops=2 * LAGS * rows * columns * count,
            bytes_accessed=4 * LAGS * rows * columns, transcendentals=0),
        name="correlate",
    )(first, second)


def solution(mesh):
    R, C = mesh.shape["row"], mesh.shape["col"]

    def on_device(traces, taps):
        count = (traces.shape[1] - taps.shape[0] + 2) // 2
        width = count - LAGS + 1
        if (R, C) == (8, 4) and traces.shape[0] == 128:
            first, second = spread(C, count, width, traces.T, taps)
            return correlate_slots(first, second, width)
        first, second = gather(R, C, count, traces, taps)
        first = first.reshape(-1, count)
        second = second.reshape(-1, count)
        return correlate(first, second, width)

    placed = (P(("row", "col"), None), P())
    return jax.shard_map(
        on_device, mesh=mesh, in_specs=placed, out_specs=P(None, "row", "col"), check_vma=False
    )
```

```python
import functools
import math

import jax
import jax.numpy as jnp
from jax import lax
from jax.experimental import pallas as pl
from jax.experimental.pallas import tpu as pltpu
from jax.sharding import PartitionSpec as P

LAGS = 32
MESH = pl.DeviceIdType.MESH


def whiten(x_ref, taps_ref, count):
    taps = taps_ref.shape[0]
    tile = 128
    depth = 2 * tile + taps - 2
    m = lax.broadcasted_iota(jnp.int32, (depth, tile), 0)
    n = lax.broadcasted_iota(jnp.int32, (depth, tile), 1)
    offset = m - 2 * n
    band = jnp.zeros((depth, tile), jnp.float32)
    for k in range(taps):
        band = jnp.where(offset == k, taps_ref[k], band)
    high = band.astype(jnp.bfloat16)
    rest = band - high.astype(jnp.float32)
    middle = rest.astype(jnp.bfloat16)
    low = (rest - middle.astype(jnp.float32)).astype(jnp.bfloat16)
    pieces = []
    for t in range(count // tile):
        x = x_ref[:, 2 * tile * t : 2 * tile * t + depth]
        total = jnp.dot(x, low, preferred_element_type=jnp.float32)
        total += jnp.dot(x, middle, preferred_element_type=jnp.float32)
        total += jnp.dot(x, high, preferred_element_type=jnp.float32)
        pieces.append(total)
    decimated = jnp.concatenate(pieces, axis=1)
    centred = decimated - jnp.mean(decimated, axis=1, keepdims=True)
    spread = jnp.sqrt(jnp.mean(centred * centred, axis=1, keepdims=True) + 1e-06)
    return (centred / spread).astype(jnp.bfloat16)


def gather_kernel(R, C, count, x_ref, taps_ref, first, second, send1, recv1, send2, recv2, sendp, recvp):
    r = lax.axis_index("row")
    c = lax.axis_index("col")
    block = r * C + c
    to_r, to_c = lax.rem(block, R), lax.div(block, R)
    wanted = c * R + r
    from_r, from_c = lax.div(wanted, C), lax.rem(wanted, C)
    fixed = wanted == block

    barrier = pltpu.get_barrier_semaphore()

    def greet(row, col):
        pl.semaphore_signal(barrier, inc=1, device_id=(row, col), device_id_type=MESH)

    for k in range(1, R):
        greet(lax.rem(r + k, R), c)
    for k in range(1, C):
        greet(r, lax.rem(c + k, C))

    @pl.when(jnp.logical_not(fixed))
    def _():
        greet(to_r, to_c)
        greet(from_r, from_c)

    mine = whiten(x_ref, taps_ref, count)
    first[pl.ds(c, 1)] = mine[None]

    @pl.when(fixed)
    def _():
        second[pl.ds(r, 1)] = mine[None]

    pl.semaphore_wait(barrier, R - 1 + C - 1 + jnp.where(fixed, 0, 2))

    def swap():
        return pltpu.make_async_remote_copy(
            first.at[c], second.at[to_r], sendp, recvp, device_id=(to_r, to_c), device_id_type=MESH)

    def arrived_swap():
        return pltpu.make_async_remote_copy(
            first.at[c], second.at[r], sendp, recvp, device_id=(to_r, to_c), device_id_type=MESH)

    def col_copy(slot, col, way):
        return pltpu.make_async_remote_copy(
            first.at[slot], first.at[slot], send1.at[way, slot], recv1.at[slot],
            device_id=(r, col), device_id_type=MESH)

    def row_copy(slot, row, k):
        return pltpu.make_async_remote_copy(
            second.at[slot], second.at[slot], send2.at[k], recv2.at[slot],
            device_id=(row, c), device_id_type=MESH)

    @pl.when(jnp.logical_not(fixed))
    def _():
        swap().start()

    @pl.when(c + 1 < C)
    def _():
        col_copy(c, c + 1, 0).start()

    @pl.when(c >= 1)
    def _():
        col_copy(c, c - 1, 1).start()

    @pl.when(jnp.logical_not(fixed))
    def _():
        arrived_swap().wait_recv()

    half = R // 2
    core = lax.rem(r, 2)
    chip = lax.div(r, 2)
    partner = r + 1 - 2 * core
    for k in list(range(1, half)):
        row_copy(r, 2 * lax.rem(chip + k, half) + core, k).start()
    row_copy(r, partner, 0).start()

    for step in range(1, max(half, C)):
        if step < C:
            left, right = c - step, c + step

            @pl.when(left >= 0)
            def _():
                col_copy(left, c, 0).wait_recv()

                @pl.when(c + 1 < C)
                def _():
                    col_copy(left, c + 1, 0).start()

            @pl.when(right < C)
            def _():
                col_copy(right, c, 1).wait_recv()

                @pl.when(c >= 1)
                def _():
                    col_copy(right, c - 1, 1).start()

        if step < half:
            slot = 2 * lax.rem(chip + half - step, half) + core
            row_copy(slot, partner, 0).wait_recv()
            row_copy(slot, partner, half + step).start()

    for k in range(half):
        slot = 2 * lax.rem(chip + k, half) + 1 - core
        row_copy(slot, partner, 0).wait_recv()

    for k in range(half):
        row_copy(r, partner, k).wait_send()
    for k in range(1, half):
        row_copy(r, partner, half + k).wait_send()

    @pl.when(jnp.logical_not(fixed))
    def _():
        swap().wait_send()

    for slot in range(C):
        @pl.when(jnp.logical_and(slot <= c, c + 1 < C))
        def _():
            col_copy(slot, c + 1, 0).wait_send()

        @pl.when(jnp.logical_and(slot >= c, c >= 1))
        def _():
            col_copy(slot, c - 1, 1).wait_send()


def gather(R, C, count, traces, taps):
    rows = traces.shape[0]
    vmem = pl.BlockSpec(memory_space=pltpu.VMEM)
    return pl.pallas_call(
        functools.partial(gather_kernel, R, C, count),
        out_shape=(
            jax.ShapeDtypeStruct((C, rows, count), jnp.bfloat16),
            jax.ShapeDtypeStruct((R, rows, count), jnp.bfloat16),
        ),
        in_specs=[vmem, pl.BlockSpec(memory_space=pltpu.SMEM)],
        out_specs=(vmem, vmem),
        scratch_shapes=[
            pltpu.SemaphoreType.DMA((2, C)),
            pltpu.SemaphoreType.DMA((C,)),
            pltpu.SemaphoreType.DMA((R,)),
            pltpu.SemaphoreType.DMA((R,)),
            pltpu.SemaphoreType.DMA,
            pltpu.SemaphoreType.DMA,
        ],
        compiler_params=pltpu.CompilerParams(
            collective_id=0, has_side_effects=True, vmem_limit_bytes=32 * 1024 * 1024),
        name="whiten_gather",
    )(traces, taps)


def correlate_kernel(width, per_step, first, second, out, left, right, lagged):
    rows = left.shape[0]

    @pl.when(pl.program_id(0) == 0)
    def _():
        n = lax.broadcasted_iota(jnp.int32, left.shape, 1)
        left[...] = jnp.where(n < width, first[...].astype(jnp.float32), 0.0)
        right[...] = second[...].T

    scale = 1.0 / math.sqrt(width)
    x = left[...]
    for k in range(per_step):
        lagged[k * rows : (k + 1) * rows] = x.astype(jnp.bfloat16)
        x = pltpu.roll(x, 1, 1)
    left[...] = x
    product = jnp.dot(lagged[...], right[...], preferred_element_type=jnp.float32) * scale
    out[...] = product.reshape(out.shape)


def correlate(first, second, width, per_step=4):
    rows, count = first.shape
    columns = second.shape[0]
    return pl.pallas_call(
        functools.partial(correlate_kernel, width, per_step),
        out_shape=jax.ShapeDtypeStruct((LAGS, rows, columns), jnp.float32),
        grid=(LAGS // per_step,),
        in_specs=[
            pl.BlockSpec((rows, count), lambda s: (0, 0)),
            pl.BlockSpec((columns, count), lambda s: (0, 0)),
        ],
        out_specs=pl.BlockSpec((per_step, rows, columns), lambda s: (s, 0, 0)),
        scratch_shapes=[
            pltpu.VMEM((rows, count), jnp.float32),
            pltpu.VMEM((count, columns), jnp.bfloat16),
            pltpu.VMEM((per_step * rows, count), jnp.bfloat16),
        ],
        compiler_params=pltpu.CompilerParams(vmem_limit_bytes=48 * 1024 * 1024),
        cost_estimate=pl.CostEstimate(
            flops=2 * LAGS * rows * columns * count,
            bytes_accessed=4 * LAGS * rows * columns, transcendentals=0),
        name="correlate",
    )(first, second)


def whiten_columns(x, taps_ref, count):
    taps = taps_ref.shape[0]
    tile = 128
    depth = 2 * tile + taps - 2
    n = lax.broadcasted_iota(jnp.int32, (tile, depth), 0)
    m = lax.broadcasted_iota(jnp.int32, (tile, depth), 1)
    offset = m - 2 * n
    band = jnp.zeros((tile, depth), jnp.float32)
    for k in range(taps):
        band = jnp.where(offset == k, taps_ref[k], band)
    high = band.astype(jnp.bfloat16)
    rest = band - high.astype(jnp.float32)
    middle = rest.astype(jnp.bfloat16)
    low = (rest - middle.astype(jnp.float32)).astype(jnp.bfloat16)
    pieces = []
    for t in range(count // tile):
        part = x[2 * tile * t : 2 * tile * t + depth]
        total = jnp.dot(low, part, preferred_element_type=jnp.float32)
        total += jnp.dot(middle, part, preferred_element_type=jnp.float32)
        total += jnp.dot(high, part, preferred_element_type=jnp.float32)
        pieces.append(total)
    decimated = jnp.concatenate(pieces, axis=0)
    centred = decimated - jnp.mean(decimated, axis=0, keepdims=True)
    spread = jnp.sqrt(jnp.mean(centred * centred, axis=0, keepdims=True) + 1e-06)
    return (centred / spread).astype(jnp.bfloat16)


def spread_kernel(C, count, width, parts, x_hbm, taps_hbm, first, second, column, carry, x_ref, taps_ref,
                  in_sem, send_z, recv_z, send_p, recv_p, send_c, recv_c,
                  send_a, recv_a, send_b):
    r = lax.axis_index("row")
    c = lax.axis_index("col")
    core = lax.rem(r, 2)
    place = lax.div(r, 2)
    px, py = lax.rem(place, 2), lax.div(place, 2)
    beside = 2 * (2 * py + 1 - px) + core
    across = 2 * (2 * (1 - py) + px) + core
    partner = r + 1 - 2 * core
    source = place == c
    sx, sy = lax.rem(c, 2), lax.div(c, 2)
    same_x, same_y = px == sx, py == sy
    corner = jnp.logical_and(jnp.logical_not(same_x), jnp.logical_not(same_y))
    near = jnp.logical_and(jnp.logical_not(source), jnp.logical_not(corner))
    relay_y = jnp.logical_and(jnp.logical_and(near, same_y), core == 0)
    relay_x = jnp.logical_and(jnp.logical_and(near, same_x), core == 1)
    far = C - 1 - c
    ends = jnp.logical_or(c == 0, far == 0)
    starts = jnp.logical_and(ends, corner)
    carries = jnp.logical_and(ends, jnp.logical_not(corner))
    relay = jnp.logical_or(relay_x, relay_y)
    passes = jnp.where(core == 0, across, beside)
    along_x = jnp.logical_and(near, same_y)
    along_y = jnp.logical_and(near, same_x)
    mine, other = core * C, (1 - core) * C
    depth = count // parts

    read_x = pltpu.make_async_copy(x_hbm, x_ref, in_sem.at[0])
    read_taps = pltpu.make_async_copy(taps_hbm, taps_ref, in_sem.at[1])
    read_x.start()
    read_taps.start()

    barrier = pltpu.get_barrier_semaphore()

    def greet(row, col):
        pl.semaphore_signal(barrier, inc=1, device_id=(row, col), device_id_type=MESH)

    greet(partner, c)

    @pl.when(jnp.logical_or(along_x, jnp.logical_and(along_y, ends)))
    def _():
        greet(beside, c)

    @pl.when(jnp.logical_or(along_y, jnp.logical_and(along_x, ends)))
    def _():
        greet(across, c)

    @pl.when(corner)
    def _():
        greet(passes, c)

    @pl.when(c + 1 < C)
    def _():
        greet(r, c + 1)

    @pl.when(c >= 1)
    def _():
        greet(r, c - 1)

    @pl.when(jnp.logical_and(ends, jnp.logical_not(source)))
    def _():
        greet(r, far)

    @pl.when(jnp.logical_and(ends, source))
    def _():
        greet(2 * far + core, c)

    read_taps.wait()
    read_x.wait()
    block = whiten_columns(x_ref[...], taps_ref, count)
    column[pl.ds(c, 1)] = block[None]

    @pl.when(source)
    def _():
        second[pl.ds(mine + c, 1)] = block[None]

    pl.semaphore_wait(
        barrier, 1 + jnp.where(c + 1 < C, 1, 0) + jnp.where(c >= 1, 1, 0) + jnp.where(carries, 1, 0)
        + jnp.where(starts, 3, 0) + jnp.where(source, 2, 0) + jnp.where(relay, 1, 0))

    def rows_of(part):
        return pl.ds(pl.multiple_of(part * depth, depth), depth)

    def z_copy(slot, part, col, way):
        ref = column.at[slot, rows_of(part)]
        return pltpu.make_async_remote_copy(
            ref, ref, send_z.at[way, slot, part], recv_z.at[slot, part],
            device_id=(r, col), device_id_type=MESH)

    def plane_copy(buffer, index, slot, part, row, way):
        return pltpu.make_async_remote_copy(
            buffer.at[index, rows_of(part)], second.at[mine + slot, rows_of(part)],
            send_p.at[way, slot, part], recv_p.at[slot, part],
            device_id=(row, c), device_id_type=MESH)

    def core_copy(buffer, index, slot, part):
        return pltpu.make_async_remote_copy(
            buffer.at[index, rows_of(part)], second.at[mine + slot, rows_of(part)],
            send_c.at[slot, part], recv_c.at[slot, part],
            device_id=(partner, c), device_id_type=MESH)

    def core_arrived(slot, part):
        ref = second.at[other + slot, rows_of(part)]
        return pltpu.make_async_remote_copy(
            ref, ref, send_c.at[slot, part], recv_c.at[slot, part],
            device_id=(partner, c), device_id_type=MESH)

    def carry_start(part, way):
        ref = column.at[c, rows_of(part)]
        return pltpu.make_async_remote_copy(
            ref, carry.at[rows_of(part)], send_a.at[way, part], recv_a.at[part],
            device_id=((beside, across, 2 * c + core)[way], c), device_id_type=MESH)

    def carry_on(part):
        return pltpu.make_async_remote_copy(
            carry.at[rows_of(part)], second.at[mine + c, rows_of(part)], send_b.at[part], recv_p.at[c, part],
            device_id=(r, far), device_id_type=MESH)

    def spread_out(slot, part, step):
        @pl.when(source)
        def _():
            if step < C - 1:
                plane_copy(column, slot, slot, part, beside, 0).start()
                plane_copy(column, slot, slot, part, across, 1).start()
            core_copy(column, slot, slot, part).start()

    def hear(slot, part, step):
        plane_copy(column, slot, slot, part, beside, 0).wait_recv()

        if step < C - 1:
            @pl.when(relay_y)
            def _():
                plane_copy(second, mine + slot, slot, part, across, 1).start()

            @pl.when(relay_x)
            def _():
                plane_copy(second, mine + slot, slot, part, beside, 0).start()

        core_copy(second, mine + slot, slot, part).start()

    def each(step, act):
        if step == 0:
            act(c)
            return

        @pl.when(c - step >= 0)
        def _():
            act(c - step)

        @pl.when(c + step < C)
        def _():
            act(c + step)

    def keep(slot):
        @pl.when(source)
        def _():
            second[pl.ds(mine + slot, 1)] = column[pl.ds(slot, 1)]

    def turn(slot):
        block = column[pl.ds(slot, 1)][0].astype(jnp.float32)
        n = lax.broadcasted_iota(jnp.int32, block.shape, 0)
        rows = block.shape[1]
        turned = jnp.where(n < width, block, 0.0).T.astype(jnp.bfloat16)
        first[pl.ds(pl.multiple_of(slot * rows, rows), rows)] = turned

    @pl.loop(0, parts)
    def _(part):
        @pl.when(c + 1 < C)
        def _():
            z_copy(c, part, c + 1, 0).start()

        @pl.when(c >= 1)
        def _():
            z_copy(c, part, c - 1, 1).start()

        spread_out(c, part, 0)

        @pl.when(starts)
        def _():
            for way in range(3):
                carry_start(part, way).start()

    turn(c)

    for step in range(1, C + 2):
        if step == 1:
            @pl.when(carries)
            def _():
                @pl.loop(0, parts)
                def _(part):
                    carry_start(part, 0).wait_recv()
                    carry_on(part).start()

        @pl.loop(0, parts)
        def _(part):
            if step < C:
                @pl.when(c - step >= 0)
                def _():
                    z_copy(c - step, part, c, 0).wait_recv()

                    @pl.when(c + 1 < C)
                    def _():
                        z_copy(c - step, part, c + 1, 0).start()

                    spread_out(c - step, part, step)

                @pl.when(c + step < C)
                def _():
                    z_copy(c + step, part, c, 1).wait_recv()

                    @pl.when(c >= 1)
                    def _():
                        z_copy(c + step, part, c - 1, 1).start()

                    spread_out(c + step, part, step)

            if step - 1 < C:
                @pl.when(near)
                def _():
                    each(step - 1, lambda slot: hear(slot, part, step - 1))

            if step >= 2:
                @pl.when(corner)
                def _():
                    each(step - 2, lambda slot: hear(slot, part, step - 2))

        if step < C:
            each(step, keep)
            each(step, turn)

    @pl.loop(0, C * parts)
    def _(k):
        slot, part = lax.div(k, parts), lax.rem(k, parts)
        core_arrived(slot, part).wait_recv()
        core_copy(column, slot, slot, part).wait_send()

        near_slot = jnp.logical_and(slot - c < C - 1, c - slot < C - 1)

        @pl.when(jnp.logical_and(near_slot, jnp.logical_or(source, relay_x)))
        def _():
            plane_copy(column, slot, slot, part, beside, 0).wait_send()

        @pl.when(jnp.logical_and(near_slot, jnp.logical_or(source, relay_y)))
        def _():
            plane_copy(column, slot, slot, part, across, 1).wait_send()

        @pl.when(jnp.logical_and(slot <= c, c + 1 < C))
        def _():
            z_copy(slot, part, c + 1, 0).wait_send()

        @pl.when(jnp.logical_and(slot >= c, c >= 1))
        def _():
            z_copy(slot, part, c - 1, 1).wait_send()

    @pl.loop(0, parts)
    def _(part):
        @pl.when(starts)
        def _():
            for way in range(3):
                carry_start(part, way).wait_send()

        @pl.when(carries)
        def _():
            carry_on(part).wait_send()


def spread(C, count, width, columns, taps, parts=2):
    rows = columns.shape[1]
    vmem = pl.BlockSpec(memory_space=pltpu.VMEM)
    hbm = pl.BlockSpec(memory_space=pltpu.HBM)
    return pl.pallas_call(
        functools.partial(spread_kernel, C, count, width, parts),
        out_shape=(
            jax.ShapeDtypeStruct((C * rows, count), jnp.bfloat16),
            jax.ShapeDtypeStruct((2 * C, count, rows), jnp.bfloat16),
        ),
        in_specs=[hbm, hbm],
        out_specs=(vmem, vmem),
        scratch_shapes=[
            pltpu.VMEM((C, count, rows), jnp.bfloat16),
            pltpu.VMEM((count, rows), jnp.bfloat16),
            pltpu.VMEM(columns.shape, columns.dtype),
            pltpu.SMEM(taps.shape, taps.dtype),
            pltpu.SemaphoreType.DMA((2,)),
            pltpu.SemaphoreType.DMA((2, C, parts)),
            pltpu.SemaphoreType.DMA((C, parts)),
            pltpu.SemaphoreType.DMA((2, C, parts)),
            pltpu.SemaphoreType.DMA((C, parts)),
            pltpu.SemaphoreType.DMA((C, parts)),
            pltpu.SemaphoreType.DMA((C, parts)),
            pltpu.SemaphoreType.DMA((3, parts)),
            pltpu.SemaphoreType.DMA((parts,)),
            pltpu.SemaphoreType.DMA((parts,)),
        ],
        compiler_params=pltpu.CompilerParams(
            collective_id=1, has_side_effects=True, vmem_limit_bytes=16 * 1024 * 1024),
        name="whiten_spread",
    )(columns, taps)


def correlate_slots_kernel(width, per_step, first, second, out, left, right, lagged, done, single, sem, sem_single, sem_half):
    rows = left.shape[0]
    steps = LAGS // per_step - 2
    slots = done.shape[0]
    for k in range(second.shape[0]):
        right[:, k * second.shape[2] : (k + 1) * second.shape[2]] = second[k]
    scale = 1.0 / math.sqrt(width)

    def products(lags):
        x = left[...]
        for k in range(lags):
            lagged[k * rows : (k + 1) * rows] = x.astype(jnp.bfloat16)
            x = pltpu.roll(x, 1, 1)
        left[...] = x
        result = jnp.dot(lagged[: lags * rows], right[...], preferred_element_type=jnp.float32) * scale
        return result.reshape((lags,) + done.shape[2:])

    def store(step, slot):
        return pltpu.make_async_copy(
            done.at[slot], out.at[pl.ds(per_step * (step + 1), per_step)], sem.at[slot])

    def store_single(lag, slot):
        return pltpu.make_async_copy(single.at[slot], out.at[lag], sem_single.at[slot])

    def store_half(half):
        part = pl.ds(half * (rows // 2), rows // 2)
        return pltpu.make_async_copy(single.at[0, part], out.at[0, part], sem_half.at[half])

    for half in range(2):
        part = slice(half * (rows // 2), (half + 1) * (rows // 2))
        single[0, part] = jnp.dot(first[part], right[...], preferred_element_type=jnp.float32) * scale
        store_half(half).start()
    left[...] = pltpu.roll(first[...].astype(jnp.float32), 1, 1)
    for k in range(1, per_step):
        single[k] = products(1)[0]
        store_single(k, k).start()

    @pl.loop(0, steps)
    def _(step):
        slot = lax.rem(step, slots)

        @pl.when(step >= slots)
        def _():
            store(step - slots, slot).wait()

        done[pl.ds(slot, 1)] = products(per_step)[None]
        store(step, slot).start()

    for k in range(per_step):
        if k == 0:
            store_half(0).wait()
            store_half(1).wait()
        else:
            store_single(k, k).wait()
        single[k] = products(1)[0]
        store_single(LAGS - per_step + k, k).start()
    for step in range(steps - slots, steps):
        store(step, step % slots).wait()
    for k in range(per_step):
        store_single(LAGS - per_step + k, k).wait()


def correlate_slots(first, second, width, per_step=2, slots=3):
    rows, count = first.shape
    columns = second.shape[0] * second.shape[2]
    vmem = pl.BlockSpec(memory_space=pltpu.VMEM)
    return pl.pallas_call(
        functools.partial(correlate_slots_kernel, width, per_step),
        out_shape=jax.ShapeDtypeStruct((LAGS, rows, columns), jnp.float32),
        in_specs=[vmem, vmem],
        out_specs=pl.BlockSpec(memory_space=pl.ANY),
        scratch_shapes=[
            pltpu.VMEM((rows, count), jnp.float32),
            pltpu.VMEM((count, columns), jnp.bfloat16),
            pltpu.VMEM((per_step * rows, count), jnp.bfloat16),
            pltpu.VMEM((slots, per_step, rows, columns), jnp.float32),
            pltpu.VMEM((per_step, rows, columns), jnp.float32),
            pltpu.SemaphoreType.DMA((slots,)),
            pltpu.SemaphoreType.DMA((per_step,)),
            pltpu.SemaphoreType.DMA((2,)),
        ],
        compiler_params=pltpu.CompilerParams(vmem_limit_bytes=48 * 1024 * 1024),
        cost_estimate=pl.CostEstimate(
            flops=2 * LAGS * rows * columns * count,
            bytes_accessed=4 * LAGS * rows * columns, transcendentals=0),
        name="correlate",
    )(first, second)


def solution(mesh):
    R, C = mesh.shape["row"], mesh.shape["col"]

    def on_device(traces, taps):
        count = (traces.shape[1] - taps.shape[0] + 2) // 2
        width = count - LAGS + 1
        if (R, C) == (8, 4) and traces.shape[0] == 128:
            first, second = spread(C, count, width, traces.T, taps)
            return correlate_slots(first, second, width)
        first, second = gather(R, C, count, traces, taps)
        first = first.reshape(-1, count)
        second = second.reshape(-1, count)
        return correlate(first, second, width)

    placed = (P(("row", "col"), None), P())
    return jax.shard_map(
        on_device, mesh=mesh, in_specs=placed, out_specs=P(None, "row", "col"), check_vma=False
    )
```
